512 devices in a mesh: row: 32 (over z, core), col: 16 (over x, y).
Axes of the slice: x: 4, y: 4, z: 16, core: 2. Of those that a mesh axis runs over, the one named last changes fastest.
Arguments:
- locations: int32 [1, 16384], P(None, 'row'), may hold values from 0 to 65535, as said below
- scales: float32 [1, 16384], P(None, 'row'), may hold values from 0.5 to 2
- sample_times: int32 [1, 16384], P(None, 'row'), may hold values from 0 to 2047
Outputs:
- factored: bfloat16 [1, 16384, 2, 8192], P(None, 'row', None, 'col')
The draws below stay inside these ranges and needn't reach their ends.
Inputs may be any that keep to these rules, and one draw needn't show every extreme that they name: `locations`: distinct Morton codes of cells of a 256 by 256 grid, increasing in row-major order; the first and last cells are always among them.
All inputs are finite; a program needn't handle non-finite values.
Results may differ from the reference program's by a relative error of at most 0.007.
Values may be sent and summed in bfloat16 or wider, within the bound.
No kernel may reach another device: no remote copies, remote signals or barrier semaphores. Data moves between devices by JAX's collectives and lax.ppermute only.
A program may use at most 64 MiB of HBM per device.

```python
import math
import jax
import jax.numpy as jnp
from jax import lax

NB = 512
ORDER = 16384
PANELS = 2
GRID = 256
TILES = 32
ROW_ROUNDS = 1
ROW_SPAN = 16384
COL_ROUNDS = 2
COL_SPAN = 8192
TIME_STEPS = 2048


def draw_locations(key, part):
    key = jax.random.fold_in(key, 7)
    inner = jax.random.permutation(key, GRID * GRID - 2)[:ORDER - 2].astype(jnp.int32) + 1
    chosen = jnp.concatenate([jnp.zeros((1,), jnp.int32), inner, jnp.full((1,), GRID * GRID - 1, jnp.int32)])
    return jnp.sort(chosen).reshape(ROW_ROUNDS, ROW_SPAN)


def place_ends(entries, rng, low, largest):
    longest = entries.shape.index(max(entries.shape))
    spots = []
    for shift in (0, 1):
        where = [jax.random.randint(jax.random.fold_in(rng, axis), (), 0, length) for axis, length in enumerate(entries.shape)]
        where[longest] = (where[longest] + shift) % entries.shape[longest]
        spots.append(tuple(where))
    return entries.at[spots[0]].set(low).at[spots[1]].set(largest)


def level_of(rng, dims, cuts, low, top_value):
    gain, own = 1.0, jax.random.fold_in(rng, 6)
    for position, parts in cuts:
        draws = jnp.exp(jax.random.uniform(jax.random.fold_in(own, position), (parts,), jnp.float32, low / len(cuts), top_value / len(cuts)))
        gain = gain * jnp.repeat(draws, dims[position] // parts).reshape([-1 if axis == position else 1 for axis in range(len(dims))])
    return gain


def setup_inputs(seed: int = 0) -> dict:
    splits = jax.random.split(jax.random.key(seed), 4)
    return {
        "locations": draw_locations(jax.random.fold_in(splits[3], 71), 0),
        "scales": jnp.clip(jnp.exp(math.log(2.0) - 1.3862944 * jax.random.uniform(splits[1], (ROW_ROUNDS, ROW_SPAN), jnp.float32) ** level_of(splits[1], (ROW_ROUNDS, ROW_SPAN), ((1, 32),), -0.2, 0.2)), 0.5, 2.0),
        "sample_times": place_ends(jax.random.randint(splits[2], (ROW_ROUNDS, ROW_SPAN), 0, TIME_STEPS), jax.random.fold_in(splits[2], 1), 0, TIME_STEPS - 1).astype(jnp.int32),
    }


RANGE_LENGTH = 0.3
TIME_RANGE = 8.0
NUGGET = 1.0

def decode_points(locations):
    bit_count = GRID.bit_length() - 1
    across = jnp.zeros_like(locations)
    upward = jnp.zeros_like(locations)
    for bit_level in range(bit_count):
        across = across + locations // 4 ** bit_level % 2 * 2 ** bit_level
        upward = upward + locations // (2 * 4 ** bit_level) % 2 * 2 ** bit_level
    return ((across.astype(jnp.float32) + 0.5) / GRID, (upward.astype(jnp.float32) + 0.5) / GRID)

def covariance(first, second, self_pairs):
    delta_x = first[0][..., :, None] - second[0][..., None, :]
    delta_y = first[1][..., :, None] - second[1][..., None, :]
    delta_t = first[2][..., :, None] - second[2][..., None, :]
    distance = jnp.sqrt(delta_x * delta_x + delta_y * delta_y)
    decay_term = jnp.exp(-(distance / RANGE_LENGTH + jnp.abs(delta_t) / TIME_RANGE))
    if self_pairs is not None:
        decay_term = jnp.where(self_pairs, decay_term + NUGGET, decay_term)
    return first[3][..., :, None] * second[3][..., None, :] * decay_term

def rounded(values):
    return lax.optimization_barrier(values.astype(jnp.bfloat16)).astype(jnp.float32)

def product(left, right):
    return lax.dot_general(left.astype(jnp.float32), right.astype(jnp.float32), (((1,), (1,)), ((), ())), preferred_element_type=jnp.float32)

def reference(locations, scales, sample_times):
    across, upward = decode_points(locations.reshape(ORDER))
    moments = sample_times.reshape(ORDER).astype(jnp.float32)
    points = (across, upward, moments, scales.reshape(ORDER))
    tile_of = jnp.arange(ORDER, dtype=jnp.int32) // NB
    panels = []
    factors = []
    for panel_index in range(PANELS):
        start_row = panel_index * NB
        picked = tuple((values[start_row:start_row + NB] for values in points))
        self_pairs = jnp.arange(ORDER, dtype=jnp.int32)[:, None] == start_row + jnp.arange(NB, dtype=jnp.int32)[None, :]
        column = covariance(points, picked, self_pairs)
        on_diagonal = (tile_of == panel_index)[:, None]
        column = jnp.where(on_diagonal, column, rounded(column))
        for earlier in panels:
            update = product(earlier, earlier[start_row:start_row + NB])
            column = jnp.where(on_diagonal, column - update, rounded(column - update))
        factor = jnp.linalg.cholesky(column[start_row:start_row + NB])
        solved = lax.linalg.triangular_solve(factor, column, left_side=False, lower=True, transpose_a=True)
        panel = jnp.where((tile_of > panel_index)[:, None], solved, 0.0).astype(jnp.bfloat16)
        panels.append(panel)
        factors.append(factor)

    def one_row(tile_index):
        start_row = tile_index * NB
        picked = tuple((lax.dynamic_slice_in_dim(values, start_row, NB) for values in points))
        self_pairs = (start_row + jnp.arange(NB, dtype=jnp.int32))[:, None] == jnp.arange(ORDER, dtype=jnp.int32)[None, :]
        row_block = covariance(picked, points, self_pairs)
        diagonal_columns = (tile_of == tile_index)[None, :]
        row_block = jnp.where(diagonal_columns, row_block, rounded(row_block))
        for panel in panels:
            own_tiles = lax.dynamic_slice_in_dim(panel, start_row, NB)
            update = product(own_tiles, panel)
            row_block = jnp.where(diagonal_columns, row_block - update, rounded(row_block - update))
        for panel_index in range(PANELS):
            own_tiles = lax.dynamic_slice_in_dim(panels[panel_index], start_row, NB).astype(jnp.float32)
            replacement = jnp.where(tile_index > panel_index, own_tiles, jnp.where(tile_index == panel_index, factors[panel_index], jnp.zeros_like(own_tiles)))
            row_block = row_block.at[:, panel_index * NB:(panel_index + 1) * NB].set(replacement)
        above_band = (tile_index < PANELS) & (tile_of[None, :] > tile_index)
        row_block = jnp.where(above_band, jnp.zeros_like(row_block), row_block)
        return row_block.astype(jnp.bfloat16)
    row_blocks = lax.map(one_row, jnp.arange(TILES, dtype=jnp.int32))
    return row_blocks.reshape(ROW_ROUNDS, ROW_SPAN, COL_ROUNDS, COL_SPAN)
```

```python
import functools

import jax
import jax.numpy as jnp
from jax import lax
from jax.experimental import pallas as pl
from jax.experimental.pallas import tpu as pltpu
from jax.sharding import PartitionSpec as P

NB = 512
BLOCK = 128
STEP = 16
PANELS = 2
GRID = 256
RANGE_LENGTH = 0.3
TIME_RANGE = 8.0
NUGGET = 1.0
LOG2E = 1.4426950408889634
HIGH = lax.Precision.HIGH
F32 = jnp.float32
BF16 = jnp.bfloat16


def dot_nt(a, b, precision=None):
    return lax.dot_general(
        a, b, (((1,), (1,)), ((), ())), preferred_element_type=F32, precision=precision
    )


def dot_nn(a, b, precision=None):
    return lax.dot_general(
        a, b, (((1,), (0,)), ((), ())), preferred_element_type=F32, precision=precision
    )


def lane_column(value, column):
    return jnp.broadcast_to(value[:, column : column + 1], (8, BLOCK))


def sublane_row(value, row):
    return jnp.broadcast_to(value[row : row + 1, :], (8, BLOCK))


def inverse_factor(block):
    groups = BLOCK // 8
    sub = lax.broadcasted_iota(jnp.int32, (8, BLOCK), 0)
    lane = lax.broadcasted_iota(jnp.int32, (8, BLOCK), 1)
    unit = [jnp.where(sub == r, 1.0, 0.0).astype(F32) for r in range(8)]
    rows = [block[8 * g : 8 * g + 8, :] for g in range(groups)]
    result = []
    for step in range(BLOCK // STEP):
        first = step * STEP
        top = first // 8
        inside = (lane >= first) & (lane < first + STEP)
        columns = [[lane_column(rows[top + a], first + c) for a in range(2)] for c in range(STEP)]
        pivot = [
            jnp.where(inside, jnp.where(lane - first == sub + 8 * a, 1.0, 0.0), rows[top + a])
            for a in range(2)
        ]
        done = [jnp.zeros((8, BLOCK), F32), jnp.zeros((8, BLOCK), F32)]
        for pair in range(STEP // 2):
            c0, c1 = 2 * pair, 2 * pair + 1
            a, r0, r1 = c0 // 8, c0 % 8, c1 % 8
            d00 = sublane_row(columns[c0][a], r0)
            d01 = sublane_row(columns[c1][a], r0)
            d11 = sublane_row(columns[c1][a], r1)
            scale = 1.0 / (d00 * d11 - d01 * d01)
            w0 = [columns[c0][g] - unit[r0] if g == a else columns[c0][g] for g in range(2)]
            w1 = [columns[c1][g] - unit[r1] if g == a else columns[c1][g] for g in range(2)]

            def sweep(z):
                z0, z1 = sublane_row(z[a], r0), sublane_row(z[a], r1)
                y0 = (d11 * z0 - d01 * z1) * scale
                y1 = (d00 * z1 - d01 * z0) * scale
                return [z[g] - (w0[g] * y0 + w1[g] * y1) for g in range(2)], z0, z1

            for c in range(c1 + 1, STEP):
                columns[c], _, _ = sweep(columns[c])
            pivot, z0, z1 = sweep(pivot)
            ratio = d01 / d00
            x0 = z0 * lax.rsqrt(d00)
            x1 = (z1 - z0 * ratio) * lax.rsqrt(d11 - d01 * ratio)
            done[a] = jnp.where(sub == r0, x0, jnp.where(sub == r1, x1, done[a]))
        result += done
        if step == BLOCK // STEP - 1:
            break
        near = range(top + 2, top + 4)
        old = list(rows)
        for h in near:
            total = jnp.where(inside, 0.0, old[h])
            parts = [
                lane_column(old[h], first + c) * sublane_row(pivot[c // 8], c % 8)
                for c in range(STEP)
            ]
            while len(parts) > 1:
                parts = [parts[i] + parts[i + 1] for i in range(0, len(parts), 2)]
            rows[h] = total - parts[0]
        if top + 4 < groups:
            below = jnp.concatenate(old[top + 4 :], axis=0)
            spread = jnp.concatenate(
                ([jnp.zeros((first, BLOCK), F32)] if first else [])
                + pivot
                + [jnp.zeros((BLOCK - first - STEP, BLOCK), F32)],
                axis=0,
            )
            change = dot_nn(below, spread, HIGH)
            for h in range(top + 4, groups):
                k = h - top - 4
                rows[h] = jnp.where(inside, 0.0, old[h]) - change[8 * k : 8 * k + 8, :]
    out = jnp.concatenate(result, axis=0)
    r = lax.broadcasted_iota(jnp.int32, (BLOCK, BLOCK), 0)
    c = lax.broadcasted_iota(jnp.int32, (BLOCK, BLOCK), 1)
    return jnp.where(c <= r, out, 0.0)


def tile_kernel(
    place_ref, gathered_ref, out_ref,
    lanes, subs, schur, lower, inverse, high, low, current, unit_inverse, factors,
    first_panel, cov, panels,
):
    row_tile = place_ref[0]
    col_tile = place_ref[1]
    second_col = place_ref[2]
    ids = (0, 1, row_tile, col_tile, second_col)

    for slot, tile in enumerate(ids):
        raw = gathered_ref[tile]
        codes = raw[0:1, :].astype(jnp.int32)
        across = jnp.zeros_like(codes)
        upward = jnp.zeros_like(codes)
        for bit in range(GRID.bit_length() - 1):
            across = across + (((codes >> (2 * bit)) & 1) << bit)
            upward = upward + (((codes >> (2 * bit + 1)) & 1) << bit)
        step = LOG2E / (RANGE_LENGTH * GRID)
        x = across.astype(F32) * step
        y = upward.astype(F32) * step
        t = raw[1:2, :] * (LOG2E / TIME_RANGE)
        s = raw[2:3, :]
        stacked = jnp.concatenate([x, y, t, s, jnp.zeros((4, NB), F32)], axis=0)
        lanes[:, slot * NB : (slot + 1) * NB] = stacked
        for q in range(NB // BLOCK):
            part = stacked[:, q * BLOCK : (q + 1) * BLOCK]
            subs[slot * NB + q * BLOCK : slot * NB + (q + 1) * BLOCK, :] = part.T

    def covariance(row_start, row_count, col_start):
        rows = pl.ds(row_start, row_count)
        cols = pl.ds(col_start, NB)
        dx = subs[rows, 0:1] - lanes[0:1, cols]
        dy = subs[rows, 1:2] - lanes[1:2, cols]
        dt = subs[rows, 2:3] - lanes[2:3, cols]
        square = dx * dx + dy * dy
        length = square * lax.rsqrt(jnp.maximum(square, 1e-30))
        decay = jnp.exp2(-(length + jnp.abs(dt)))
        return decay, subs[rows, 3:4] * lanes[3:4, cols]

    def own_pairs(start, count):
        r = lax.broadcasted_iota(jnp.int32, (count, NB), 0) + start
        c = lax.broadcasted_iota(jnp.int32, (count, NB), 1)
        return r == c

    chunk = 64

    def fill_offdiagonal(row_slot, col_slot):
        @pl.loop(0, NB // chunk)
        def _(i):
            start = pl.multiple_of(i * chunk, chunk)
            decay, gain = covariance(
                pl.multiple_of(row_slot * NB + start, chunk), chunk, col_slot * NB
            )
            cov[pl.ds(start, chunk), :] = (decay * gain).astype(BF16)

    def fill_diagonal(slot, change):
        @pl.loop(0, NB // chunk)
        def _(i):
            start = pl.multiple_of(i * chunk, chunk)
            decay, gain = covariance(
                pl.multiple_of(slot * NB + start, chunk), chunk, slot * NB
            )
            decay = jnp.where(own_pairs(start, chunk), decay + NUGGET, decay)
            value = decay * gain
            if change:
                value = value - schur[pl.ds(start, chunk), :]
            schur[pl.ds(start, chunk), :] = value

    def solve(values, panel):
        half = NB // 2
        left = values[:, :half]
        parts = [
            dot_nt(left, high[panel, :half, :half]) + dot_nt(left, low[panel, :half, :half]),
            dot_nt(values, high[panel, half:, :]) + dot_nt(values, low[panel, half:, :]),
        ]
        return jnp.concatenate(parts, axis=1).astype(BF16)

    fill_diagonal(0, False)
    current[...] = schur[0:BLOCK, 0:BLOCK]
    factors[...] = jnp.zeros_like(factors)
    is_factor = (row_tile == col_tile) & (row_tile < PANELS)

    def stage(panel, part):
        begin, end = part * BLOCK, (part + 1) * BLOCK
        inv = unit_inverse[...]
        inverse[begin:end, begin:end] = inv

        @pl.when(is_factor & (row_tile == panel))
        def _():
            factors[begin:end, begin:end] = dot_nt(current[...], inv, HIGH).astype(BF16)

        if end < NB:
            solved = dot_nt(schur[end:, begin:end], inv, HIGH)
            lower[end:, begin:end] = solved

            @pl.when(is_factor & (row_tile == panel))
            def _():
                factors[end:, begin:end] = solved.astype(BF16)

            top = solved[:BLOCK]
            current[...] = schur[end : end + BLOCK, end : end + BLOCK] - dot_nt(top, top, HIGH)
            for q in range(end, NB, BLOCK):
                here = solved[q - end : q - end + BLOCK]
                schur[q:, q : q + BLOCK] = schur[q:, q : q + BLOCK] - dot_nt(
                    solved[q - end :], here, HIGH
                )
        else:
            half = NB // 2
            for q in (0, half):
                m = q + BLOCK
                e = q + half
                inverse[m:e, q:m] = -dot_nn(
                    inverse[m:e, m:e], dot_nn(lower[m:e, q:m], inverse[q:m, q:m], HIGH), HIGH
                )
                inverse[q:m, m:e] = jnp.zeros((BLOCK, BLOCK), F32)
            inverse[half:, :half] = -dot_nn(
                inverse[half:, half:], dot_nn(lower[half:, :half], inverse[:half, :half], HIGH), HIGH
            )
            inverse[:half, half:] = jnp.zeros((half, half), F32)
            whole = inverse[...]
            head = whole.astype(BF16)
            high[panel] = head
            low[panel] = (whole - head.astype(F32)).astype(BF16)
            if panel + 1 < PANELS:
                fill_offdiagonal(1, 0)
                solved = solve(cov[...], 0)
                first_panel[...] = solved
                schur[...] = dot_nt(solved, solved)
                fill_diagonal(1, True)
                current[...] = schur[0:BLOCK, 0:BLOCK]

    parts = NB // BLOCK

    @pl.loop(0, PANELS * parts)
    def _(index):
        unit_inverse[...] = inverse_factor(current[...])
        for k in range(PANELS * parts):
            pl.when(index == k)(functools.partial(stage, k // parts, k % parts))

    @pl.loop(0, 3)
    def _(k):
        slot = 2 + k
        place = pl.ds(pl.multiple_of(k * NB, NB), NB)
        fill_offdiagonal(slot, 0)
        solved = solve(cov[...], 0)
        panels[0, place, :] = solved
        fill_offdiagonal(slot, 1)
        reduced = (cov[...].astype(F32) - dot_nt(solved, first_panel[...])).astype(BF16)
        panels[1, place, :] = solve(reduced, 1)

    for k in range(2):
        tile = ids[3 + k]

        @pl.when((row_tile < PANELS) & (tile > row_tile))
        def _():
            out_ref[k] = jnp.zeros((NB, NB), BF16)

        @pl.when((row_tile >= PANELS) & (tile >= PANELS))
        def _():
            col_place = pl.ds((1 + k) * NB, NB)

            @pl.loop(0, NB // BLOCK)
            def _(i):
                start = pl.multiple_of(i * BLOCK, BLOCK)
                decay, gain = covariance(
                    pl.multiple_of(2 * NB + start, BLOCK), BLOCK, (3 + k) * NB
                )
                held = tile == row_tile
                decay = jnp.where(own_pairs(start, BLOCK) & held, decay + NUGGET, decay)
                value = decay * gain

                def kept(v):
                    return jnp.where(held, v, v.astype(BF16).astype(F32))

                value = kept(value)
                for panel in range(PANELS):
                    change = dot_nt(panels[panel, pl.ds(start, BLOCK), :], panels[panel, col_place, :])
                    value = kept(value - change)
                out_ref[k, pl.ds(start, BLOCK), :] = value.astype(BF16)

    for panel in range(PANELS):

        @pl.when((col_tile == panel) & (row_tile > panel))
        def _():
            out_ref[0] = panels[panel, 0:NB, :]

    @pl.when(is_factor)
    def _():
        r = lax.broadcasted_iota(jnp.int32, (NB, NB), 0)
        c = lax.broadcasted_iota(jnp.int32, (NB, NB), 1)
        out_ref[0] = jnp.where(c <= r, factors[...].astype(F32), 0.0).astype(BF16)


def device_tiles(place, gathered):
    vmem = pl.BlockSpec(memory_space=pltpu.VMEM)
    return pl.pallas_call(
        tile_kernel,
        out_shape=jax.ShapeDtypeStruct((2, NB, NB), BF16),
        in_specs=[pl.BlockSpec(memory_space=pltpu.SMEM), vmem],
        out_specs=vmem,
        scratch_shapes=[
            pltpu.VMEM((8, 5 * NB), F32),
            pltpu.VMEM((5 * NB, 8), F32),
            pltpu.VMEM((NB, NB), F32),
            pltpu.VMEM((NB, NB), F32),
            pltpu.VMEM((NB, NB), F32),
            pltpu.VMEM((PANELS, NB, NB), BF16),
            pltpu.VMEM((PANELS, NB, NB), BF16),
            pltpu.VMEM((BLOCK, BLOCK), F32),
            pltpu.VMEM((BLOCK, BLOCK), F32),
            pltpu.VMEM((NB, NB), BF16),
            pltpu.VMEM((NB, NB), BF16),
            pltpu.VMEM((NB, NB), BF16),
            pltpu.VMEM((PANELS, 3 * NB, NB), BF16),
        ],
        compiler_params=pltpu.CompilerParams(vmem_limit_bytes=48 * 1024 * 1024),
    )(place, gathered)


def per_device(locations, scales, sample_times):
    row_place = lax.axis_index("row")
    col_place = lax.axis_index("col")
    own = jnp.stack([locations.astype(F32), sample_times.astype(F32), scales], axis=1)
    gathered = lax.all_gather(own, "row", axis=0, tiled=True)
    place = jnp.stack([row_place, col_place, col_place + lax.axis_size("col")]).astype(jnp.int32)
    tiles = device_tiles(place, gathered)
    return jnp.transpose(tiles, (1, 0, 2))[None]


def solution(mesh):
    return jax.shard_map(
        per_device,
        mesh=mesh,
        in_specs=(P(None, "row"), P(None, "row"), P(None, "row")),
        out_specs=P(None, "row", None, "col"),
        check_vma=False,
    )
```

```python
import functools

import jax
import jax.numpy as jnp
from jax import lax
from jax.experimental import pallas as pl
from jax.experimental.pallas import tpu as pltpu
from jax.sharding import PartitionSpec as P

NB = 512
BLOCK = 128
STEP = 16
PANELS = 2
GRID = 256
RANGE_LENGTH = 0.3
TIME_RANGE = 8.0
NUGGET = 1.0
LOG2E = 1.4426950408889634
HIGH = lax.Precision.HIGH
F32 = jnp.float32
BF16 = jnp.bfloat16


def dot_nt(a, b, precision=None):
    return lax.dot_general(
        a, b, (((1,), (1,)), ((), ())), preferred_element_type=F32, precision=precision
    )


def dot_nn(a, b, precision=None):
    return lax.dot_general(
        a, b, (((1,), (0,)), ((), ())), preferred_element_type=F32, precision=precision
    )


def lane_column(value, column):
    return jnp.broadcast_to(value[:, column : column + 1], (8, BLOCK))


def sublane_row(value, row):
    return jnp.broadcast_to(value[row : row + 1, :], (8, BLOCK))


def pairwise_sum(parts):
    while len(parts) > 1:
        parts = [sum(parts[i : i + 2][1:], parts[i]) for i in range(0, len(parts), 2)]
    return parts[0]


def inverse_factor(block):
    groups = BLOCK // 8
    deep = STEP // 8
    sub = lax.broadcasted_iota(jnp.int32, (8, BLOCK), 0)
    lane = lax.broadcasted_iota(jnp.int32, (8, BLOCK), 1)
    unit = [jnp.where(sub == r, 1.0, 0.0).astype(F32) for r in range(8)]
    rows = [block[8 * g : 8 * g + 8, :] for g in range(groups)]
    result = []
    for first in range(0, BLOCK, STEP):
        top = first // 8
        inside = (lane >= first) & (lane < first + STEP)
        columns = [
            [lane_column(rows[top + g], first + c) for g in range(deep)] for c in range(STEP)
        ]
        pivot = [
            jnp.where(inside, jnp.where(lane - first == sub + 8 * g, 1.0, 0.0), rows[top + g])
            for g in range(deep)
        ]
        done = [jnp.zeros((8, BLOCK), F32) for _ in range(deep)]
        for c0 in range(0, STEP, 2):
            c1 = c0 + 1
            a, r0, r1 = c0 // 8, c0 % 8, c1 % 8
            d00 = sublane_row(columns[c0][a], r0)
            d01 = sublane_row(columns[c1][a], r0)
            d11 = sublane_row(columns[c1][a], r1)
            scale = 1.0 / (d00 * d11 - d01 * d01)
            w0 = [columns[c0][g] - unit[r0] if g == a else columns[c0][g] for g in range(deep)]
            w1 = [columns[c1][g] - unit[r1] if g == a else columns[c1][g] for g in range(deep)]
            m0 = [(d11 * columns[c0][g] - d01 * columns[c1][g]) * scale for g in range(a, deep)]
            m1 = [(d00 * columns[c1][g] - d01 * columns[c0][g]) * scale for g in range(a, deep)]
            for c in range(c1 + 1, STEP):
                y0 = sublane_row(m0[c // 8 - a], c % 8)
                y1 = sublane_row(m1[c // 8 - a], c % 8)
                columns[c] = [columns[c][g] - (w0[g] * y0 + w1[g] * y1) for g in range(deep)]
            z0, z1 = sublane_row(pivot[a], r0), sublane_row(pivot[a], r1)
            y0 = (d11 * z0 - d01 * z1) * scale
            y1 = (d00 * z1 - d01 * z0) * scale
            pivot = [pivot[g] - (w0[g] * y0 + w1[g] * y1) for g in range(deep)]
            ratio = d01 / d00
            x0 = z0 * lax.rsqrt(d00)
            x1 = (z1 - z0 * ratio) * lax.rsqrt(d11 - d01 * ratio)
            done[a] = jnp.where(sub == r0, x0, jnp.where(sub == r1, x1, done[a]))
        result += done
        if first + STEP == BLOCK:
            break
        old = list(rows)
        for h in range(top + deep, top + 2 * deep):
            parts = [
                lane_column(old[h], first + c) * sublane_row(pivot[c // 8], c % 8)
                for c in range(STEP)
            ]
            rows[h] = jnp.where(inside, 0.0, old[h]) - pairwise_sum(parts)
        far = top + 2 * deep
        if far < groups:
            below = jnp.concatenate(old[far:], axis=0)
            spread = jnp.concatenate(
                ([jnp.zeros((first, BLOCK), F32)] if first else [])
                + pivot
                + [jnp.zeros((BLOCK - first - STEP, BLOCK), F32)],
                axis=0,
            )
            change = dot_nn(below, spread, HIGH)
            for h in range(far, groups):
                k = 8 * (h - far)
                rows[h] = jnp.where(inside, 0.0, old[h]) - change[k : k + 8, :]
    out = jnp.concatenate(result, axis=0)
    r = lax.broadcasted_iota(jnp.int32, (BLOCK, BLOCK), 0)
    c = lax.broadcasted_iota(jnp.int32, (BLOCK, BLOCK), 1)
    return jnp.where(c <= r, out, 0.0)


def tile_kernel(
    place_ref, gathered_ref, out_ref,
    lanes, subs, schur, lower, inverse, high, low, current, unit_inverse, factors,
    first_panel, cov, panels,
):
    row_tile = place_ref[0]
    col_tile = place_ref[1]
    second_col = place_ref[2]
    ids = (0, 1, row_tile, col_tile, second_col)

    for slot, tile in enumerate(ids):
        raw = gathered_ref[tile]
        codes = raw[0:1, :].astype(jnp.int32)
        across = jnp.zeros_like(codes)
        upward = jnp.zeros_like(codes)
        for bit in range(GRID.bit_length() - 1):
            across = across + (((codes >> (2 * bit)) & 1) << bit)
            upward = upward + (((codes >> (2 * bit + 1)) & 1) << bit)
        step = LOG2E / (RANGE_LENGTH * GRID)
        x = across.astype(F32) * step
        y = upward.astype(F32) * step
        t = raw[1:2, :] * (LOG2E / TIME_RANGE)
        s = raw[2:3, :]
        stacked = jnp.concatenate([x, y, t, s, jnp.zeros((4, NB), F32)], axis=0)
        lanes[:, slot * NB : (slot + 1) * NB] = stacked
        for q in range(NB // BLOCK):
            part = stacked[:, q * BLOCK : (q + 1) * BLOCK]
            subs[slot * NB + q * BLOCK : slot * NB + (q + 1) * BLOCK, :] = part.T

    def covariance(row_start, row_count, col_start):
        rows = pl.ds(row_start, row_count)
        cols = pl.ds(col_start, NB)
        dx = subs[rows, 0:1] - lanes[0:1, cols]
        dy = subs[rows, 1:2] - lanes[1:2, cols]
        dt = subs[rows, 2:3] - lanes[2:3, cols]
        square = dx * dx + dy * dy
        length = square * lax.rsqrt(jnp.maximum(square, 1e-30))
        decay = jnp.exp2(-(length + jnp.abs(dt)))
        return decay, subs[rows, 3:4] * lanes[3:4, cols]

    def own_pairs(start, count):
        r = lax.broadcasted_iota(jnp.int32, (count, NB), 0) + start
        c = lax.broadcasted_iota(jnp.int32, (count, NB), 1)
        return r == c

    chunk = 256

    def fill_offdiagonal(row_slot, col_slot):
        @pl.loop(0, NB // chunk)
        def _(i):
            start = pl.multiple_of(i * chunk, chunk)
            decay, gain = covariance(
                pl.multiple_of(row_slot * NB + start, chunk), chunk, col_slot * NB
            )
            cov[pl.ds(start, chunk), :] = (decay * gain).astype(BF16)

    def fill_diagonal(slot, change):
        @pl.loop(0, NB // chunk)
        def _(i):
            start = pl.multiple_of(i * chunk, chunk)
            decay, gain = covariance(
                pl.multiple_of(slot * NB + start, chunk), chunk, slot * NB
            )
            decay = jnp.where(own_pairs(start, chunk), decay + NUGGET, decay)
            value = decay * gain
            if change:
                value = value - schur[pl.ds(start, chunk), :]
            schur[pl.ds(start, chunk), :] = value

    def solve(values, panel):
        half = NB // 2
        left = values[:, :half]
        parts = [
            dot_nt(left, high[panel, :half, :half]) + dot_nt(left, low[panel, :half, :half]),
            dot_nt(values, high[panel, half:, :]) + dot_nt(values, low[panel, half:, :]),
        ]
        return jnp.concatenate(parts, axis=1).astype(BF16)

    fill_diagonal(0, False)
    current[...] = schur[0:BLOCK, 0:BLOCK]
    factors[...] = jnp.zeros_like(factors)
    is_factor = (row_tile == col_tile) & (row_tile < PANELS)

    def stage(panel, part):
        begin, end = part * BLOCK, (part + 1) * BLOCK
        inv = unit_inverse[...]
        inverse[begin:end, begin:end] = inv

        @pl.when(is_factor & (row_tile == panel))
        def _():
            factors[begin:end, begin:end] = dot_nt(current[...], inv, HIGH).astype(BF16)

        if end < NB:
            solved = dot_nt(schur[end:, begin:end], inv, HIGH)
            lower[end:, begin:end] = solved

            @pl.when(is_factor & (row_tile == panel))
            def _():
                factors[end:, begin:end] = solved.astype(BF16)

            top = solved[:BLOCK]
            current[...] = schur[end : end + BLOCK, end : end + BLOCK] - dot_nt(top, top, HIGH)
            for q in range(end, NB, BLOCK):
                here = solved[q - end : q - end + BLOCK]
                schur[q:, q : q + BLOCK] = schur[q:, q : q + BLOCK] - dot_nt(
                    solved[q - end :], here, HIGH
                )
        else:
            half = NB // 2
            for q in (0, half):
                m = q + BLOCK
                e = q + half
                inverse[m:e, q:m] = -dot_nn(
                    inverse[m:e, m:e], dot_nn(lower[m:e, q:m], inverse[q:m, q:m], HIGH), HIGH
                )
                inverse[q:m, m:e] = jnp.zeros((BLOCK, BLOCK), F32)
            inverse[half:, :half] = -dot_nn(
                inverse[half:, half:], dot_nn(lower[half:, :half], inverse[:half, :half], HIGH), HIGH
            )
            inverse[:half, half:] = jnp.zeros((half, half), F32)
            whole = inverse[...]
            head = whole.astype(BF16)
            high[panel] = head
            low[panel] = (whole - head.astype(F32)).astype(BF16)
            if panel + 1 < PANELS:
                fill_offdiagonal(1, 0)
                solved = solve(cov[...], 0)
                first_panel[...] = solved
                schur[...] = dot_nt(solved, solved)
                fill_diagonal(1, True)
                current[...] = schur[0:BLOCK, 0:BLOCK]

    parts = NB // BLOCK

    @pl.loop(0, PANELS * parts)
    def _(index):
        unit_inverse[...] = inverse_factor(current[...])
        for k in range(PANELS * parts):
            pl.when(index == k)(functools.partial(stage, k // parts, k % parts))

    @pl.loop(0, 3 * NB // chunk)
    def _(i):
        start = pl.multiple_of(2 * NB + i * chunk, chunk)
        place = pl.ds(pl.multiple_of(i * chunk, chunk), chunk)
        decay, gain = covariance(start, chunk, 0)
        solved = solve((decay * gain).astype(BF16), 0)
        panels[0, place, :] = solved
        decay, gain = covariance(start, chunk, NB)
        value = (decay * gain).astype(BF16).astype(F32) - dot_nt(solved, first_panel[...])
        panels[1, place, :] = solve(value.astype(BF16), 1)

    for k in range(2):
        tile = ids[3 + k]

        @pl.when((row_tile < PANELS) & (tile > row_tile))
        def _():
            out_ref[k] = jnp.zeros((NB, NB), BF16)

        @pl.when((row_tile >= PANELS) & (tile >= PANELS))
        def _():
            col_place = pl.ds((1 + k) * NB, NB)

            @pl.loop(0, NB // chunk)
            def _(i):
                start = pl.multiple_of(i * chunk, chunk)
                decay, gain = covariance(
                    pl.multiple_of(2 * NB + start, chunk), chunk, (3 + k) * NB
                )
                held = tile == row_tile
                decay = jnp.where(own_pairs(start, chunk) & held, decay + NUGGET, decay)
                value = decay * gain

                def kept(v):
                    return jnp.where(held, v, v.astype(BF16).astype(F32))

                value = kept(value)
                for panel in range(PANELS):
                    change = dot_nt(panels[panel, pl.ds(start, chunk), :], panels[panel, col_place, :])
                    value = kept(value - change)
                out_ref[k, pl.ds(start, chunk), :] = value.astype(BF16)

    for panel in range(PANELS):

        @pl.when((col_tile == panel) & (row_tile > panel))
        def _():
            out_ref[0] = panels[panel, 0:NB, :]

    @pl.when(is_factor)
    def _():
        r = lax.broadcasted_iota(jnp.int32, (NB, NB), 0)
        c = lax.broadcasted_iota(jnp.int32, (NB, NB), 1)
        out_ref[0] = jnp.where(c <= r, factors[...].astype(F32), 0.0).astype(BF16)


def device_tiles(place, gathered):
    vmem = pl.BlockSpec(memory_space=pltpu.VMEM)
    return pl.pallas_call(
        tile_kernel,
        out_shape=jax.ShapeDtypeStruct((2, NB, NB), BF16),
        in_specs=[pl.BlockSpec(memory_space=pltpu.SMEM), vmem],
        out_specs=vmem,
        scratch_shapes=[
            pltpu.VMEM((8, 5 * NB), F32),
            pltpu.VMEM((5 * NB, 8), F32),
            pltpu.VMEM((NB, NB), F32),
            pltpu.VMEM((NB, NB), F32),
            pltpu.VMEM((NB, NB), F32),
            pltpu.VMEM((PANELS, NB, NB), BF16),
            pltpu.VMEM((PANELS, NB, NB), BF16),
            pltpu.VMEM((BLOCK, BLOCK), F32),
            pltpu.VMEM((BLOCK, BLOCK), F32),
            pltpu.VMEM((NB, NB), BF16),
            pltpu.VMEM((NB, NB), BF16),
            pltpu.VMEM((NB, NB), BF16),
            pltpu.VMEM((PANELS, 3 * NB, NB), BF16),
        ],
        compiler_params=pltpu.CompilerParams(vmem_limit_bytes=48 * 1024 * 1024),
    )(place, gathered)


def per_device(locations, scales, sample_times):
    row_place = lax.axis_index("row")
    col_place = lax.axis_index("col")
    own = jnp.stack([locations.astype(F32), sample_times.astype(F32), scales], axis=1)
    gathered = lax.all_gather(own, "row", axis=0, tiled=True)
    place = jnp.stack([row_place, col_place, col_place + lax.axis_size("col")]).astype(jnp.int32)
    tiles = device_tiles(place, gathered)
    return jnp.transpose(tiles, (1, 0, 2))[None]


def solution(mesh):
    return jax.shard_map(
        per_device,
        mesh=mesh,
        in_specs=(P(None, "row"), P(None, "row"), P(None, "row")),
        out_specs=P(None, "row", None, "col"),
        check_vma=False,
    )
```

```python
import functools

import jax
import jax.numpy as jnp
from jax import lax
from jax.experimental import pallas as pl
from jax.experimental.pallas import tpu as pltpu
from jax.sharding import PartitionSpec as P

NB = 512
BLOCK = 128
STEP = 16
PANELS = 2
GRID = 256
RANGE_LENGTH = 0.3
TIME_RANGE = 8.0
NUGGET = 1.0
LOG2E = 1.4426950408889634
MID_TIME = 1024.0
HIGH = lax.Precision.HIGH
F32 = jnp.float32
BF16 = jnp.bfloat16


def dot_nt(a, b, precision=None):
    return lax.dot_general(
        a, b, (((1,), (1,)), ((), ())), preferred_element_type=F32, precision=precision
    )


def dot_nn(a, b, precision=None):
    return lax.dot_general(
        a, b, (((1,), (0,)), ((), ())), preferred_element_type=F32, precision=precision
    )


def lane_column(value, column):
    return jnp.broadcast_to(value[:, column : column + 1], (8, BLOCK))


def sublane_row(value, row):
    return jnp.broadcast_to(value[row : row + 1, :], (8, BLOCK))


def pairwise_sum(parts):
    while len(parts) > 1:
        parts = [sum(parts[i : i + 2][1:], parts[i]) for i in range(0, len(parts), 2)]
    return parts[0]


def inverse_factor(block):
    groups = BLOCK // 8
    deep = STEP // 8
    sub = lax.broadcasted_iota(jnp.int32, (8, BLOCK), 0)
    lane = lax.broadcasted_iota(jnp.int32, (8, BLOCK), 1)
    unit = [jnp.where(sub == r, 1.0, 0.0).astype(F32) for r in range(8)]
    rows = [block[8 * g : 8 * g + 8, :] for g in range(groups)]
    result = []
    for first in range(0, BLOCK, STEP):
        top = first // 8
        inside = (lane >= first) & (lane < first + STEP)
        columns = [
            [lane_column(rows[top + g], first + c) for g in range(deep)] for c in range(STEP)
        ]
        pivot = [
            jnp.where(inside, jnp.where(lane - first == sub + 8 * g, 1.0, 0.0), rows[top + g])
            for g in range(deep)
        ]
        done = [jnp.zeros((8, BLOCK), F32) for _ in range(deep)]
        for c0 in range(0, STEP, 2):
            c1 = c0 + 1
            a, r0, r1 = c0 // 8, c0 % 8, c1 % 8
            d00 = sublane_row(columns[c0][a], r0)
            d01 = sublane_row(columns[c1][a], r0)
            d11 = sublane_row(columns[c1][a], r1)
            scale = 1.0 / (d00 * d11 - d01 * d01)
            w0 = [columns[c0][g] - unit[r0] if g == a else columns[c0][g] for g in range(deep)]
            w1 = [columns[c1][g] - unit[r1] if g == a else columns[c1][g] for g in range(deep)]
            m0 = [(d11 * columns[c0][g] - d01 * columns[c1][g]) * scale for g in range(a, deep)]
            m1 = [(d00 * columns[c1][g] - d01 * columns[c0][g]) * scale for g in range(a, deep)]
            for c in range(c1 + 1, STEP):
                y0 = sublane_row(m0[c // 8 - a], c % 8)
                y1 = sublane_row(m1[c // 8 - a], c % 8)
                columns[c] = [columns[c][g] - (w0[g] * y0 + w1[g] * y1) for g in range(deep)]
            z0, z1 = sublane_row(pivot[a], r0), sublane_row(pivot[a], r1)
            y0 = (d11 * z0 - d01 * z1) * scale
            y1 = (d00 * z1 - d01 * z0) * scale
            pivot = [pivot[g] - (w0[g] * y0 + w1[g] * y1) for g in range(deep)]
            ratio = d01 / d00
            x0 = z0 * lax.rsqrt(d00)
            x1 = (z1 - z0 * ratio) * lax.rsqrt(d11 - d01 * ratio)
            done[a] = jnp.where(sub == r0, x0, jnp.where(sub == r1, x1, done[a]))
        result += done
        if first + STEP == BLOCK:
            break
        old = list(rows)
        for h in range(top + deep, top + 2 * deep):
            parts = [
                lane_column(old[h], first + c) * sublane_row(pivot[c // 8], c % 8)
                for c in range(STEP)
            ]
            rows[h] = jnp.where(inside, 0.0, old[h]) - pairwise_sum(parts)
        far = top + 2 * deep
        if far < groups:
            below = jnp.concatenate(old[far:], axis=0)
            spread = jnp.concatenate(
                ([jnp.zeros((first, BLOCK), F32)] if first else [])
                + pivot
                + [jnp.zeros((BLOCK - first - STEP, BLOCK), F32)],
                axis=0,
            )
            change = dot_nn(below, spread, HIGH)
            for h in range(far, groups):
                k = 8 * (h - far)
                rows[h] = jnp.where(inside, 0.0, old[h]) - change[k : k + 8, :]
    out = jnp.concatenate(result, axis=0)
    r = lax.broadcasted_iota(jnp.int32, (BLOCK, BLOCK), 0)
    c = lax.broadcasted_iota(jnp.int32, (BLOCK, BLOCK), 1)
    return jnp.where(c <= r, out, 0.0)


def tile_kernel(
    place_ref, gathered_ref, out_ref,
    lanes, subs, schur, lower, high, low, current, unit_inverse, pending,
    first_panel, next_panel, next_diagonal, covs, panels,
):
    row_tile = place_ref[0]
    col_tile = place_ref[1]
    second_col = place_ref[2]
    ids = (0, 1, row_tile, col_tile, second_col)

    for slot, tile in enumerate(ids):
        raw = gathered_ref[tile]
        codes = raw[0:1, :].astype(jnp.int32)
        across = jnp.zeros_like(codes)
        upward = jnp.zeros_like(codes)
        for bit in range(GRID.bit_length() - 1):
            across = across + (((codes >> (2 * bit)) & 1) << bit)
            upward = upward + (((codes >> (2 * bit + 1)) & 1) << bit)
        step = LOG2E / (RANGE_LENGTH * GRID)
        x = across.astype(F32) * step
        y = upward.astype(F32) * step
        t = (raw[1:2, :] - MID_TIME) * (LOG2E / TIME_RANGE)
        s = raw[2:3, :]
        level = jnp.log(s) * LOG2E
        stacked = jnp.concatenate([x, y, t, s, level + t, level - t, x, y], axis=0)
        lanes[:, slot * NB : (slot + 1) * NB] = stacked
        for q in range(NB // BLOCK):
            part = stacked[:, q * BLOCK : (q + 1) * BLOCK]
            subs[slot * NB + q * BLOCK : slot * NB + (q + 1) * BLOCK, :] = part.T

    def covariance(row_start, row_count, col_start):
        rows = pl.ds(row_start, row_count)
        cols = pl.ds(col_start, NB)
        dx = subs[rows, 0:1] - lanes[0:1, cols]
        dy = subs[rows, 1:2] - lanes[1:2, cols]
        dt = subs[rows, 2:3] - lanes[2:3, cols]
        square = dx * dx + dy * dy
        length = square * lax.rsqrt(jnp.maximum(square, 1e-30))
        decay = jnp.exp2(-(length + jnp.abs(dt)))
        return decay, subs[rows, 3:4] * lanes[3:4, cols]

    def own_pairs(start, count):
        r = lax.broadcasted_iota(jnp.int32, (count, NB), 0) + start
        c = lax.broadcasted_iota(jnp.int32, (count, NB), 1)
        return r == c

    chunk = 256

    def diagonal_rows(slot, start, count):
        decay, gain = covariance(slot * NB + start, count, slot * NB)
        return jnp.where(own_pairs(start, count), decay + NUGGET, decay) * gain

    def offdiagonal_rows(start, count, col_slot):
        rows = pl.ds(start, count)
        cols = pl.ds(col_slot * NB, NB)
        dx = subs[rows, 0:1] - lanes[0:1, cols]
        dy = subs[rows, 1:2] - lanes[1:2, cols]
        square = dx * dx + dy * dy
        level = jnp.minimum(
            subs[rows, 5:6] + lanes[4:5, cols], subs[rows, 4:5] + lanes[5:6, cols]
        )
        return jnp.exp2(level - square * lax.rsqrt(square)).astype(BF16)

    def solve(values, panel):
        half = NB // 2
        left = values[:, :half]
        parts = [
            dot_nt(left, high[panel, :half, :half]) + dot_nt(left, low[panel, :half, :half]),
            dot_nt(values, high[panel, half:, :]) + dot_nt(values, low[panel, half:, :]),
        ]
        return jnp.concatenate(parts, axis=1).astype(BF16)

    @pl.loop(0, NB // chunk)
    def _(i):
        start = pl.multiple_of(i * chunk, chunk)
        schur[pl.ds(start, chunk), :] = diagonal_rows(0, start, chunk)

    current[0, 0] = schur[0:BLOCK, 0:BLOCK]
    lower[...] = jnp.zeros_like(lower)
    high[...] = jnp.zeros_like(high)
    low[...] = jnp.zeros_like(low)
    is_factor = (row_tile == col_tile) & (row_tile < PANELS)

    def stage(panel, part):
        begin, end = part * BLOCK, (part + 1) * BLOCK
        inv = unit_inverse[panel, part]
        rest = [-dot_nn(inv, pending[:, :begin], HIGH)] if part else []
        if end < NB:
            rest = rest + [inv, jnp.zeros((BLOCK, NB - end), F32)]
        else:
            rest = rest + [inv]
        row = jnp.concatenate(rest, axis=1)
        head = row.astype(BF16)
        high[panel, begin:end, :] = head
        low[panel, begin:end, :] = (row - head.astype(F32)).astype(BF16)

        if end < NB:
            solved = dot_nt(schur[end:, begin:end], inv, HIGH)
            lower[panel, end:, begin:end] = solved

            top = solved[:BLOCK]
            current[panel, part + 1] = schur[end : end + BLOCK, end : end + BLOCK] - dot_nt(top, top, HIGH)
            for q in range(end, NB, BLOCK):
                here = solved[q - end : q - end + BLOCK]
                schur[q:, q : q + BLOCK] = schur[q:, q : q + BLOCK] - dot_nt(
                    solved[q - end :], here, HIGH
                )
        else:
            if panel + 1 < PANELS:
                solved = solve(next_panel[...], 0)
                first_panel[...] = solved
                current[panel + 1, 0] = next_diagonal[:BLOCK, :BLOCK] - dot_nt(solved[:BLOCK], solved[:BLOCK])
                schur[...] = next_diagonal[...] - dot_nt(solved, solved)

    def fill_pending(index, panel):
        row = lower[panel, index * BLOCK : (index + 1) * BLOCK, :]
        head = row.astype(BF16)
        tail = (row - head.astype(F32)).astype(BF16)
        both = jnp.concatenate([head, tail], axis=0)
        product = dot_nn(both, high[panel])
        pending[...] = product[:BLOCK] + product[BLOCK:] + dot_nn(head, low[panel])

    parts = NB // BLOCK
    share = 3 * NB // parts

    for index in range(parts):
        near = pl.ds(index * BLOCK, BLOCK)
        start = index * BLOCK
        next_panel[near, :] = offdiagonal_rows(NB + start, BLOCK, 0)
        next_diagonal[near, :] = diagonal_rows(1, start, BLOCK)
        own = index * share
        for panel in range(PANELS):
            covs[panel, pl.ds(own, share), :] = offdiagonal_rows(2 * NB + own, share, panel)
        fill_pending(index, 0)
        unit_inverse[0, index] = inverse_factor(current[0, index])
        stage(0, index)

    for index in range(parts):
        own = pl.ds(index * share, share)
        solved = solve(covs[0, own, :], 0)
        panels[0, own, :] = solved
        change = dot_nt(solved, first_panel[...])
        covs[1, own, :] = (covs[1, own, :].astype(F32) - change).astype(BF16)
        fill_pending(index, 1)
        unit_inverse[1, index] = inverse_factor(current[1, index])
        stage(1, index)

    @pl.loop(0, 3 * NB // chunk)
    def _(i):
        place = pl.ds(pl.multiple_of(i * chunk, chunk), chunk)
        panels[1, place, :] = solve(covs[1, place, :], 1)

    for k in range(2):
        tile = ids[3 + k]

        @pl.when((row_tile < PANELS) & (tile > row_tile))
        def _():
            out_ref[k] = jnp.zeros((NB, NB), BF16)

        def update(held):
            col_place = pl.ds((1 + k) * NB, NB)

            @pl.loop(0, NB // chunk)
            def _(i):
                start = pl.multiple_of(i * chunk, chunk)
                place = pl.ds(start, chunk)
                if held:
                    value = diagonal_rows(2, start, chunk)
                else:
                    value = offdiagonal_rows(2 * NB + start, chunk, 3 + k).astype(F32)
                for panel in range(PANELS):
                    value = value - dot_nt(panels[panel, place, :], panels[panel, col_place, :])
                    if not held:
                        value = value.astype(BF16).astype(F32)
                out_ref[k, place, :] = value.astype(BF16)

        inner = (row_tile >= PANELS) & (tile >= PANELS)
        pl.when(inner & (tile == row_tile))(functools.partial(update, True))
        pl.when(inner & (tile != row_tile))(functools.partial(update, False))

    for panel in range(PANELS):

        @pl.when((col_tile == panel) & (row_tile > panel))
        def _():
            out_ref[0] = panels[panel, 0:NB, :]

    for panel in range(PANELS):

        @pl.when(is_factor & (row_tile == panel))
        def _():
            out_ref[0] = lower[panel].astype(BF16)
            for p in range(parts):
                span = slice(p * BLOCK, (p + 1) * BLOCK)
                block = dot_nt(current[panel, p], unit_inverse[panel, p], HIGH)
                r = lax.broadcasted_iota(jnp.int32, (BLOCK, BLOCK), 0)
                c = lax.broadcasted_iota(jnp.int32, (BLOCK, BLOCK), 1)
                out_ref[0, span, span] = jnp.where(c <= r, block, 0.0).astype(BF16)


def device_tiles(place, gathered):
    vmem = pl.BlockSpec(memory_space=pltpu.VMEM)
    return pl.pallas_call(
        tile_kernel,
        out_shape=jax.ShapeDtypeStruct((2, NB, NB), BF16),
        in_specs=[pl.BlockSpec(memory_space=pltpu.SMEM), vmem],
        out_specs=vmem,
        scratch_shapes=[
            pltpu.VMEM((8, 5 * NB), F32),
            pltpu.VMEM((5 * NB, 8), F32),
            pltpu.VMEM((NB, NB), F32),
            pltpu.VMEM((PANELS, NB, NB), F32),
            pltpu.VMEM((PANELS, NB, NB), BF16),
            pltpu.VMEM((PANELS, NB, NB), BF16),
            pltpu.VMEM((PANELS, NB // BLOCK, BLOCK, BLOCK), F32),
            pltpu.VMEM((PANELS, NB // BLOCK, BLOCK, BLOCK), F32),
            pltpu.VMEM((BLOCK, NB), F32),
            pltpu.VMEM((NB, NB), BF16),
            pltpu.VMEM((NB, NB), BF16),
            pltpu.VMEM((NB, NB), F32),
            pltpu.VMEM((PANELS, 3 * NB, NB), BF16),
            pltpu.VMEM((PANELS, 3 * NB, NB), BF16),
        ],
        compiler_params=pltpu.CompilerParams(vmem_limit_bytes=48 * 1024 * 1024),
    )(place, gathered)


def per_device(locations, scales, sample_times):
    row_place = lax.axis_index("row")
    col_place = lax.axis_index("col")
    own = jnp.stack([locations.astype(F32), sample_times.astype(F32), scales], axis=1)
    gathered = lax.all_gather(own, "row", axis=0, tiled=True)
    place = jnp.stack([row_place, col_place, col_place + lax.axis_size("col")]).astype(jnp.int32)
    tiles = device_tiles(place, gathered)
    return jnp.transpose(tiles, (1, 0, 2))[None]


def solution(mesh):
    return jax.shard_map(
        per_device,
        mesh=mesh,
        in_specs=(P(None, "row"), P(None, "row"), P(None, "row")),
        out_specs=P(None, "row", None, "col"),
        check_vma=False,
    )
```

```python
import functools

import jax
import jax.numpy as jnp
from jax import lax
from jax.experimental import pallas as pl
from jax.experimental.pallas import tpu as pltpu
from jax.sharding import Mesh
from jax.sharding import PartitionSpec as P

NB = 512
BLOCK = 128
STEP = 16
PANELS = 2
GRID = 256
RANGE_LENGTH = 0.3
TIME_RANGE = 8.0
NUGGET = 1.0
LOG2E = 1.4426950408889634
MID_TIME = 1024.0
HIGH = lax.Precision.HIGH
F32 = jnp.float32
BF16 = jnp.bfloat16


def dot_nt(a, b, precision=None):
    return lax.dot_general(
        a, b, (((1,), (1,)), ((), ())), preferred_element_type=F32, precision=precision
    )


def dot_nn(a, b, precision=None):
    return lax.dot_general(
        a, b, (((1,), (0,)), ((), ())), preferred_element_type=F32, precision=precision
    )


def lane_column(value, column):
    return jnp.broadcast_to(value[:, column : column + 1], (8, BLOCK))


def sublane_row(value, row):
    return jnp.broadcast_to(value[row : row + 1, :], (8, BLOCK))


def pairwise_sum(parts):
    while len(parts) > 1:
        parts = [sum(parts[i : i + 2][1:], parts[i]) for i in range(0, len(parts), 2)]
    return parts[0]


def inverse_factor(block):
    groups = BLOCK // 8
    deep = STEP // 8
    sub = lax.broadcasted_iota(jnp.int32, (8, BLOCK), 0)
    lane = lax.broadcasted_iota(jnp.int32, (8, BLOCK), 1)
    unit = [jnp.where(sub == r, 1.0, 0.0).astype(F32) for r in range(8)]
    rows = [block[8 * g : 8 * g + 8, :] for g in range(groups)]
    result = []
    for first in range(0, BLOCK, STEP):
        top = first // 8
        inside = (lane >= first) & (lane < first + STEP)
        columns = [
            [lane_column(rows[top + g], first + c) for g in range(deep)] for c in range(STEP)
        ]
        pivot = [
            jnp.where(inside, jnp.where(lane - first == sub + 8 * g, 1.0, 0.0), rows[top + g])
            for g in range(deep)
        ]
        done = [jnp.zeros((8, BLOCK), F32) for _ in range(deep)]
        for c0 in range(0, STEP, 2):
            c1 = c0 + 1
            a, r0, r1 = c0 // 8, c0 % 8, c1 % 8
            d00 = sublane_row(columns[c0][a], r0)
            d01 = sublane_row(columns[c1][a], r0)
            d11 = sublane_row(columns[c1][a], r1)
            scale = 1.0 / (d00 * d11 - d01 * d01)
            w0 = [columns[c0][g] - unit[r0] if g == a else columns[c0][g] for g in range(deep)]
            w1 = [columns[c1][g] - unit[r1] if g == a else columns[c1][g] for g in range(deep)]
            m0 = [(d11 * columns[c0][g] - d01 * columns[c1][g]) * scale for g in range(a, deep)]
            m1 = [(d00 * columns[c1][g] - d01 * columns[c0][g]) * scale for g in range(a, deep)]
            for c in range(c1 + 1, STEP):
                y0 = sublane_row(m0[c // 8 - a], c % 8)
                y1 = sublane_row(m1[c // 8 - a], c % 8)
                columns[c] = [columns[c][g] - (w0[g] * y0 + w1[g] * y1) for g in range(deep)]
            z0, z1 = sublane_row(pivot[a], r0), sublane_row(pivot[a], r1)
            y0 = (d11 * z0 - d01 * z1) * scale
            y1 = (d00 * z1 - d01 * z0) * scale
            pivot = [pivot[g] - (w0[g] * y0 + w1[g] * y1) for g in range(deep)]
            ratio = d01 / d00
            x0 = z0 * lax.rsqrt(d00)
            x1 = (z1 - z0 * ratio) * lax.rsqrt(d11 - d01 * ratio)
            done[a] = jnp.where(sub == r0, x0, jnp.where(sub == r1, x1, done[a]))
        result += done
        if first + STEP == BLOCK:
            break
        old = list(rows)
        for h in range(top + deep, top + 2 * deep):
            parts = [
                lane_column(old[h], first + c) * sublane_row(pivot[c // 8], c % 8)
                for c in range(STEP)
            ]
            rows[h] = jnp.where(inside, 0.0, old[h]) - pairwise_sum(parts)
        far = top + 2 * deep
        if far < groups:
            below = jnp.concatenate(old[far:], axis=0)
            spread = jnp.concatenate(
                ([jnp.zeros((first, BLOCK), F32)] if first else [])
                + pivot
                + [jnp.zeros((BLOCK - first - STEP, BLOCK), F32)],
                axis=0,
            )
            change = dot_nn(below, spread, HIGH)
            for h in range(far, groups):
                k = 8 * (h - far)
                rows[h] = jnp.where(inside, 0.0, old[h]) - change[k : k + 8, :]
    out = jnp.concatenate(result, axis=0)
    r = lax.broadcasted_iota(jnp.int32, (BLOCK, BLOCK), 0)
    c = lax.broadcasted_iota(jnp.int32, (BLOCK, BLOCK), 1)
    return jnp.where(c <= r, out, 0.0)


def tile_kernel(
    place_ref, gathered_ref, out_ref,
    lanes, subs, schur, lower, high, low, current, unit_inverse, pending,
    first_panel, next_panel, next_diagonal, partial, covs, panels,
):
    row_tile = place_ref[0]
    col_tile = place_ref[1]
    second_col = place_ref[2]
    core = place_ref[3]
    ids = (0, 1, row_tile, col_tile, second_col)

    def covariance(row_start, row_count, col_start):
        rows = pl.ds(row_start, row_count)
        cols = pl.ds(col_start, NB)
        dx = subs[rows, 0:1] - lanes[0:1, cols]
        dy = subs[rows, 1:2] - lanes[1:2, cols]
        dt = subs[rows, 2:3] - lanes[2:3, cols]
        square = dx * dx + dy * dy
        length = square * lax.rsqrt(jnp.maximum(square, 1e-30))
        decay = jnp.exp2(-(length + jnp.abs(dt)))
        return decay, subs[rows, 3:4] * lanes[3:4, cols]

    def own_pairs(start, count):
        r = lax.broadcasted_iota(jnp.int32, (count, NB), 0) + start
        c = lax.broadcasted_iota(jnp.int32, (count, NB), 1)
        return r == c

    chunk = 256

    def diagonal_rows(slot, start, count):
        decay, gain = covariance(slot * NB + start, count, slot * NB)
        return jnp.where(own_pairs(start, count), decay + NUGGET, decay) * gain

    def offdiagonal_rows(start, count, col_slot):
        rows = pl.ds(start, count)
        cols = pl.ds(col_slot * NB, NB)
        dx = subs[rows, 0:1] - lanes[0:1, cols]
        dy = subs[rows, 1:2] - lanes[1:2, cols]
        square = dx * dx + dy * dy
        level = jnp.minimum(
            subs[rows, 5:6] + lanes[4:5, cols], subs[rows, 4:5] + lanes[5:6, cols]
        )
        return jnp.exp2(level - square * lax.rsqrt(square)).astype(BF16)

    half = NB // 2

    def half_solve(values, panel, begin):
        span, depth = slice(begin, begin + half), slice(0, begin + half)
        return dot_nt(values, high[panel, span, depth]) + dot_nt(values, low[panel, span, depth])

    def solve(values, panel):
        parts = [half_solve(values[:, :half], panel, 0), half_solve(values, panel, half)]
        return jnp.concatenate(parts, axis=1).astype(BF16)

    def diagonal_rows(slot, start, count):
        decay, gain = covariance(slot * NB + start, count, slot * NB)
        return jnp.where(own_pairs(start, count), decay + NUGGET, decay) * gain

    def offdiagonal_rows(start, count, col_slot):
        rows = pl.ds(start, count)
        cols = pl.ds(col_slot * NB, NB)
        dx = subs[rows, 0:1] - lanes[0:1, cols]
        dy = subs[rows, 1:2] - lanes[1:2, cols]
        square = dx * dx + dy * dy
        level = jnp.minimum(
            subs[rows, 5:6] + lanes[4:5, cols], subs[rows, 4:5] + lanes[5:6, cols]
        )
        return jnp.exp2(level - square * lax.rsqrt(square)).astype(BF16)

    def solve(values, panel):
        half = NB // 2
        left = values[:, :half]
        parts = [
            dot_nt(left, high[panel, :half, :half]) + dot_nt(left, low[panel, :half, :half]),
            dot_nt(values, high[panel, half:, :]) + dot_nt(values, low[panel, half:, :]),
        ]
        return jnp.concatenate(parts, axis=1).astype(BF16)

    def prepare(slot, tile):
        low_bit = lax.rem(tile, 2) if slot > 1 else tile % 2
        raw = gathered_ref[tile - low_bit + jnp.bitwise_xor(low_bit, core)]
        codes = raw[0:1, :].astype(jnp.int32)
        across = jnp.zeros_like(codes)
        upward = jnp.zeros_like(codes)
        for bit in range(GRID.bit_length() - 1):
            across = across + (((codes >> (2 * bit)) & 1) << bit)
            upward = upward + (((codes >> (2 * bit + 1)) & 1) << bit)
        step = LOG2E / (RANGE_LENGTH * GRID)
        x = across.astype(F32) * step
        y = upward.astype(F32) * step
        t = (raw[1:2, :] - MID_TIME) * (LOG2E / TIME_RANGE)
        s = raw[2:3, :]
        level = jnp.log(s) * LOG2E
        stacked = jnp.concatenate([x, y, t, s, level + t, level - t, x, y], axis=0)
        lanes[:, slot * NB : (slot + 1) * NB] = stacked
        for q in range(NB // BLOCK):
            part = stacked[:, q * BLOCK : (q + 1) * BLOCK]
            subs[slot * NB + q * BLOCK : slot * NB + (q + 1) * BLOCK, :] = part.T

    prepare(0, 0)
    for start in range(0, NB, chunk):
        schur[start : start + chunk, :] = diagonal_rows(0, start, chunk)

    current[0, 0] = schur[0:BLOCK, 0:BLOCK]
    for slot in range(1, 5):
        prepare(slot, ids[slot])
    lower[...] = jnp.zeros_like(lower)
    high[...] = jnp.zeros_like(high)
    low[...] = jnp.zeros_like(low)
    is_factor = (row_tile == col_tile) & (row_tile < PANELS)

    def stage(panel, part):
        begin, end = part * BLOCK, (part + 1) * BLOCK
        inv = unit_inverse[panel, part]
        rest = [-dot_nn(inv, pending[:, :begin], HIGH)] if part else []
        if end < NB:
            rest = rest + [inv, jnp.zeros((BLOCK, NB - end), F32)]
        else:
            rest = rest + [inv]
        row = jnp.concatenate(rest, axis=1)
        head = row.astype(BF16)
        high[panel, begin:end, :] = head
        low[panel, begin:end, :] = (row - head.astype(F32)).astype(BF16)

        if end < NB:
            solved = dot_nt(schur[end:, begin:end], inv, HIGH)
            lower[panel, end:, begin:end] = solved

            top = solved[:BLOCK]
            current[panel, part + 1] = schur[end : end + BLOCK, end : end + BLOCK] - dot_nt(top, top, HIGH)
            for q in range(end, NB, BLOCK):
                here = solved[q - end : q - end + BLOCK]
                schur[q:, q : q + BLOCK] = schur[q:, q : q + BLOCK] - dot_nt(
                    solved[q - end :], here, HIGH
                )
        else:
            if panel + 1 < PANELS:
                solved = solve(next_panel[...], 0)
                first_panel[...] = solved
                current[panel + 1, 0] = next_diagonal[:BLOCK, :BLOCK] - dot_nt(solved[:BLOCK], solved[:BLOCK])
                schur[...] = next_diagonal[...] - dot_nt(solved, solved)

    def fill_pending(index, panel):
        row = lower[panel, index * BLOCK : (index + 1) * BLOCK, :]
        head = row.astype(BF16)
        tail = (row - head.astype(F32)).astype(BF16)
        both = jnp.concatenate([head, tail], axis=0)
        product = dot_nn(both, high[panel])
        pending[...] = product[:BLOCK] + product[BLOCK:] + dot_nn(head, low[panel])

    def kept(k, value):
        return jnp.where(ids[3 + k] == row_tile, value, value.astype(BF16).astype(F32))

    parts = NB // BLOCK
    share = 3 * NB // parts

    for index in range(parts):
        near = pl.ds(index * BLOCK, BLOCK)
        start = index * BLOCK
        next_panel[near, :] = offdiagonal_rows(NB + start, BLOCK, 0)
        next_diagonal[near, :] = diagonal_rows(1, start, BLOCK)
        own = index * share
        for panel in range(PANELS):
            covs[panel, pl.ds(own, share), :] = offdiagonal_rows(2 * NB + own, share, panel)
        fill_pending(index, 0)
        unit_inverse[0, index] = inverse_factor(current[0, index])
        stage(0, index)

    for index in range(parts):
        if index < 2:
            same = ids[3 + index] == row_tile
            decay, gain = covariance(2 * NB, NB, (3 + index) * NB)
            decay = jnp.where(own_pairs(0, NB) & same, decay + NUGGET, decay)
            partial[index] = kept(index, decay * gain)
        if index < 3:
            own = pl.ds(index * NB, NB)
            solved = solve(covs[0, own, :], 0)
            panels[0, own, :] = solved
            change = dot_nt(solved, first_panel[...])
            covs[1, own, :] = (covs[1, own, :].astype(F32) - change).astype(BF16)
        else:
            panels[1, :, :half] = half_solve(covs[1, :, :half], 1, 0).astype(BF16)
            for k in range(2):
                change = dot_nt(panels[0, :NB, :], panels[0, (1 + k) * NB : (2 + k) * NB, :])
                partial[k] = kept(k, partial[k] - change)
        fill_pending(index, 1)
        unit_inverse[1, index] = inverse_factor(current[1, index])
        stage(1, index)

    panels[1, :, half:] = half_solve(covs[1], 1, half).astype(BF16)

    for k in range(2):
        tile = ids[3 + k]

        @pl.when((row_tile < PANELS) & (tile > row_tile))
        def _():
            out_ref[k] = jnp.zeros((NB, NB), BF16)

        @pl.when((row_tile >= PANELS) & (tile >= PANELS))
        def _():
            change = dot_nt(panels[1, :NB, :], panels[1, (1 + k) * NB : (2 + k) * NB, :])
            out_ref[k] = (partial[k] - change).astype(BF16)

    for panel in range(PANELS):

        @pl.when((col_tile == panel) & (row_tile > panel))
        def _():
            out_ref[0] = panels[panel, 0:NB, :]

    for panel in range(PANELS):

        @pl.when(is_factor & (row_tile == panel))
        def _():
            out_ref[0] = lower[panel].astype(BF16)
            for p in range(parts):
                span = slice(p * BLOCK, (p + 1) * BLOCK)
                block = dot_nt(current[panel, p], unit_inverse[panel, p], HIGH)
                r = lax.broadcasted_iota(jnp.int32, (BLOCK, BLOCK), 0)
                c = lax.broadcasted_iota(jnp.int32, (BLOCK, BLOCK), 1)
                out_ref[0, span, span] = jnp.where(c <= r, block, 0.0).astype(BF16)


def device_tiles(place, gathered):
    vmem = pl.BlockSpec(memory_space=pltpu.VMEM)
    return pl.pallas_call(
        tile_kernel,
        out_shape=jax.ShapeDtypeStruct((2, NB, NB), BF16),
        in_specs=[pl.BlockSpec(memory_space=pltpu.SMEM), vmem],
        out_specs=vmem,
        scratch_shapes=[
            pltpu.VMEM((8, 5 * NB), F32),
            pltpu.VMEM((5 * NB, 8), F32),
            pltpu.VMEM((NB, NB), F32),
            pltpu.VMEM((PANELS, NB, NB), F32),
            pltpu.VMEM((PANELS, NB, NB), BF16),
            pltpu.VMEM((PANELS, NB, NB), BF16),
            pltpu.VMEM((PANELS, NB // BLOCK, BLOCK, BLOCK), F32),
            pltpu.VMEM((PANELS, NB // BLOCK, BLOCK, BLOCK), F32),
            pltpu.VMEM((BLOCK, NB), F32),
            pltpu.VMEM((NB, NB), BF16),
            pltpu.VMEM((NB, NB), BF16),
            pltpu.VMEM((NB, NB), F32),
            pltpu.VMEM((2, NB, NB), F32),
            pltpu.VMEM((PANELS, 3 * NB, NB), BF16),
            pltpu.VMEM((PANELS, 3 * NB, NB), BF16),
        ],
        compiler_params=pltpu.CompilerParams(vmem_limit_bytes=48 * 1024 * 1024),
    )(place, gathered)


def per_device(locations, scales, sample_times):
    core = lax.axis_index("core")
    row_place = lax.axis_index("chip") * 2 + core
    col_place = lax.axis_index("col")
    chips = lax.axis_size("chip")
    own = jnp.stack([locations.astype(F32), sample_times.astype(F32), scales], axis=1)
    other = lax.ppermute(own, "core", [(0, 1), (1, 0)])
    pair = jnp.concatenate([own, other], axis=0)
    copies = jnp.broadcast_to(pair[None], (chips,) + pair.shape)
    gathered = lax.all_to_all(copies, "chip", 0, 0, tiled=True)
    gathered = gathered.reshape((2 * chips,) + own.shape[1:])
    place = jnp.stack([row_place, col_place, col_place + lax.axis_size("col"), core])
    tiles = device_tiles(place.astype(jnp.int32), gathered)
    return jnp.transpose(tiles, (1, 0, 2))[None]


def solution(mesh):
    rows, cols = mesh.devices.shape
    split = Mesh(mesh.devices.reshape(rows // 2, 2, cols), ("chip", "core", "col"))
    row = P(None, ("chip", "core"))
    return jax.shard_map(
        per_device,
        mesh=split,
        in_specs=(row, row, row),
        out_specs=P(None, ("chip", "core"), None, "col"),
        check_vma=False,
    )
```

```python
import functools

import jax
import jax.numpy as jnp
from jax import lax
from jax.experimental import pallas as pl
from jax.experimental.pallas import tpu as pltpu
from jax.sharding import Mesh
from jax.sharding import PartitionSpec as P

NB = 512
BLOCK = 128
STEP = 16
PANELS = 2
GRID = 256
RANGE_LENGTH = 0.3
TIME_RANGE = 8.0
NUGGET = 1.0
LOG2E = 1.4426950408889634
MID_TIME = 1024.0
HIGH = lax.Precision.HIGH
F32 = jnp.float32
BF16 = jnp.bfloat16


def dot_nt(a, b, precision=None):
    return lax.dot_general(
        a, b, (((1,), (1,)), ((), ())), preferred_element_type=F32, precision=precision
    )


def dot_nn(a, b, precision=None):
    return lax.dot_general(
        a, b, (((1,), (0,)), ((), ())), preferred_element_type=F32, precision=precision
    )


def lane_column(value, column):
    return jnp.broadcast_to(value[:, column : column + 1], (8, BLOCK))


def sublane_row(value, row):
    return jnp.broadcast_to(value[row : row + 1, :], (8, BLOCK))


def pairwise_sum(parts):
    while len(parts) > 1:
        parts = [sum(parts[i : i + 2][1:], parts[i]) for i in range(0, len(parts), 2)]
    return parts[0]


def inverse_factor(block):
    groups = BLOCK // 8
    deep = STEP // 8
    sub = lax.broadcasted_iota(jnp.int32, (8, BLOCK), 0)
    lane = lax.broadcasted_iota(jnp.int32, (8, BLOCK), 1)
    unit = [jnp.where(sub == r, 1.0, 0.0).astype(F32) for r in range(8)]
    rows = [block[8 * g : 8 * g + 8, :] for g in range(groups)]
    result = []
    for first in range(0, BLOCK, STEP):
        top = first // 8
        inside = (lane >= first) & (lane < first + STEP)
        columns = [
            [lane_column(rows[top + g], first + c) for g in range(deep)] for c in range(STEP)
        ]
        pivot = [
            jnp.where(inside, jnp.where(lane - first == sub + 8 * g, 1.0, 0.0), rows[top + g])
            for g in range(deep)
        ]
        done = [jnp.zeros((8, BLOCK), F32) for _ in range(deep)]
        for c0 in range(0, STEP, 2):
            c1 = c0 + 1
            a, r0, r1 = c0 // 8, c0 % 8, c1 % 8
            d00 = sublane_row(columns[c0][a], r0)
            d01 = sublane_row(columns[c1][a], r0)
            d11 = sublane_row(columns[c1][a], r1)
            scale = 1.0 / (d00 * d11 - d01 * d01)
            w0 = [columns[c0][g] - unit[r0] if g == a else columns[c0][g] for g in range(deep)]
            w1 = [columns[c1][g] - unit[r1] if g == a else columns[c1][g] for g in range(deep)]
            m0 = [(d11 * columns[c0][g] - d01 * columns[c1][g]) * scale for g in range(a, deep)]
            m1 = [(d00 * columns[c1][g] - d01 * columns[c0][g]) * scale for g in range(a, deep)]
            for c in range(c1 + 1, STEP):
                y0 = sublane_row(m0[c // 8 - a], c % 8)
                y1 = sublane_row(m1[c // 8 - a], c % 8)
                columns[c] = [columns[c][g] - (w0[g] * y0 + w1[g] * y1) for g in range(deep)]
            z0, z1 = sublane_row(pivot[a], r0), sublane_row(pivot[a], r1)
            y0 = (d11 * z0 - d01 * z1) * scale
            y1 = (d00 * z1 - d01 * z0) * scale
            pivot = [pivot[g] - (w0[g] * y0 + w1[g] * y1) for g in range(deep)]
            ratio = d01 / d00
            x0 = z0 * lax.rsqrt(d00)
            x1 = (z1 - z0 * ratio) * lax.rsqrt(d11 - d01 * ratio)
            done[a] = jnp.where(sub == r0, x0, jnp.where(sub == r1, x1, done[a]))
        result += done
        if first + STEP == BLOCK:
            break
        old = list(rows)
        for h in range(top + deep, top + 2 * deep):
            parts = [
                lane_column(old[h], first + c) * sublane_row(pivot[c // 8], c % 8)
                for c in range(STEP)
            ]
            rows[h] = jnp.where(inside, 0.0, old[h]) - pairwise_sum(parts)
        far = top + 2 * deep
        if far < groups:
            below = jnp.concatenate(old[far:], axis=0)
            spread = jnp.concatenate(
                ([jnp.zeros((first, BLOCK), F32)] if first else [])
                + pivot
                + [jnp.zeros((BLOCK - first - STEP, BLOCK), F32)],
                axis=0,
            )
            change = dot_nn(below, spread, HIGH)
            for h in range(far, groups):
                k = 8 * (h - far)
                rows[h] = jnp.where(inside, 0.0, old[h]) - change[k : k + 8, :]
    out = jnp.concatenate(result, axis=0)
    r = lax.broadcasted_iota(jnp.int32, (BLOCK, BLOCK), 0)
    c = lax.broadcasted_iota(jnp.int32, (BLOCK, BLOCK), 1)
    return jnp.where(c <= r, out, 0.0)


def tile_kernel(
    place_ref, gathered_ref, out_ref,
    lanes, subs, schur, lower, high, low, current, unit_inverse, pending,
    first_panel, next_panel, next_diagonal, partial, covs, panels,
):
    row_tile = place_ref[0]
    col_tile = place_ref[1]
    second_col = place_ref[2]
    core = place_ref[3]
    ids = (0, 1, row_tile, col_tile, second_col)

    def covariance(row_start, row_count, col_start):
        rows = pl.ds(row_start, row_count)
        cols = pl.ds(col_start, NB)
        dx = subs[rows, 0:1] - lanes[0:1, cols]
        dy = subs[rows, 1:2] - lanes[1:2, cols]
        dt = subs[rows, 2:3] - lanes[2:3, cols]
        square = dx * dx + dy * dy
        length = square * lax.rsqrt(jnp.maximum(square, 1e-30))
        decay = jnp.exp2(-(length + jnp.abs(dt)))
        return decay, subs[rows, 3:4] * lanes[3:4, cols]

    def own_pairs(start, count):
        r = lax.broadcasted_iota(jnp.int32, (count, NB), 0) + start
        c = lax.broadcasted_iota(jnp.int32, (count, NB), 1)
        return r == c

    chunk = 256

    def diagonal_rows(slot, start, count):
        decay, gain = covariance(slot * NB + start, count, slot * NB)
        return jnp.where(own_pairs(start, count), decay + NUGGET, decay) * gain

    def offdiagonal_rows(start, count, col_slot):
        rows = pl.ds(start, count)
        cols = pl.ds(col_slot * NB, NB)
        dx = subs[rows, 0:1] - lanes[0:1, cols]
        dy = subs[rows, 1:2] - lanes[1:2, cols]
        square = dx * dx + dy * dy
        level = jnp.minimum(
            subs[rows, 5:6] + lanes[4:5, cols], subs[rows, 4:5] + lanes[5:6, cols]
        )
        return jnp.exp2(level - square * lax.rsqrt(square)).astype(BF16)

    half = NB // 2

    def half_solve(values, panel, begin):
        span, depth = slice(begin, begin + half), slice(0, begin + half)
        return dot_nt(values, high[panel, span, depth]) + dot_nt(values, low[panel, span, depth])

    def solve(values, panel):
        parts = [half_solve(values[:, :half], panel, 0), half_solve(values, panel, half)]
        return jnp.concatenate(parts, axis=1).astype(BF16)

    def diagonal_rows(slot, start, count):
        decay, gain = covariance(slot * NB + start, count, slot * NB)
        return jnp.where(own_pairs(start, count), decay + NUGGET, decay) * gain

    def offdiagonal_rows(start, count, col_slot):
        rows = pl.ds(start, count)
        cols = pl.ds(col_slot * NB, NB)
        dx = subs[rows, 0:1] - lanes[0:1, cols]
        dy = subs[rows, 1:2] - lanes[1:2, cols]
        square = dx * dx + dy * dy
        level = jnp.minimum(
            subs[rows, 5:6] + lanes[4:5, cols], subs[rows, 4:5] + lanes[5:6, cols]
        )
        return jnp.exp2(level - square * lax.rsqrt(square)).astype(BF16)

    def solve(values, panel):
        half = NB // 2
        left = values[:, :half]
        parts = [
            dot_nt(left, high[panel, :half, :half]) + dot_nt(left, low[panel, :half, :half]),
            dot_nt(values, high[panel, half:, :]) + dot_nt(values, low[panel, half:, :]),
        ]
        return jnp.concatenate(parts, axis=1).astype(BF16)

    def prepare(slot, tile):
        low_bit = lax.rem(tile, 2) if slot > 1 else tile % 2
        raw = gathered_ref[tile - low_bit + jnp.bitwise_xor(low_bit, core)]
        codes = raw[0:1, :].astype(jnp.int32)
        across = jnp.zeros_like(codes)
        upward = jnp.zeros_like(codes)
        for bit in range(GRID.bit_length() - 1):
            across = across + (((codes >> (2 * bit)) & 1) << bit)
            upward = upward + (((codes >> (2 * bit + 1)) & 1) << bit)
        step = LOG2E / (RANGE_LENGTH * GRID)
        x = across.astype(F32) * step
        y = upward.astype(F32) * step
        t = (raw[1:2, :] - MID_TIME) * (LOG2E / TIME_RANGE)
        s = raw[2:3, :]
        level = jnp.log(s) * LOG2E
        stacked = jnp.concatenate([x, y, t, s, level + t, level - t, x, y], axis=0)
        lanes[:, slot * NB : (slot + 1) * NB] = stacked
        for q in range(NB // BLOCK):
            part = stacked[:, q * BLOCK : (q + 1) * BLOCK]
            subs[slot * NB + q * BLOCK : slot * NB + (q + 1) * BLOCK, :] = part.T

    prepare(0, 0)
    for start in range(0, NB, chunk):
        schur[start : start + chunk, :] = diagonal_rows(0, start, chunk)

    current[0, 0] = schur[0:BLOCK, 0:BLOCK]
    for slot in range(1, 5):
        prepare(slot, ids[slot])
    lower[...] = jnp.zeros_like(lower)
    high[...] = jnp.zeros_like(high)
    low[...] = jnp.zeros_like(low)
    is_factor = (row_tile == col_tile) & (row_tile < PANELS)

    def stage(panel, part):
        begin, end = part * BLOCK, (part + 1) * BLOCK
        inv = unit_inverse[panel, part]
        rest = [-dot_nn(inv, pending[:, :begin], HIGH)] if part else []
        if end < NB:
            rest = rest + [inv, jnp.zeros((BLOCK, NB - end), F32)]
        else:
            rest = rest + [inv]
        row = jnp.concatenate(rest, axis=1)
        head = row.astype(BF16)
        high[panel, begin:end, :] = head
        low[panel, begin:end, :] = (row - head.astype(F32)).astype(BF16)

        if end < NB:
            solved = dot_nt(schur[end:, begin:end], inv, HIGH)
            lower[panel, end:, begin:end] = solved

            top = solved[:BLOCK]
            current[panel, part + 1] = schur[end : end + BLOCK, end : end + BLOCK] - dot_nt(top, top, HIGH)
            for q in range(end, NB, BLOCK):
                here = solved[q - end : q - end + BLOCK]
                schur[q:, q : q + BLOCK] = schur[q:, q : q + BLOCK] - dot_nt(
                    solved[q - end :], here, HIGH
                )
        else:
            if panel + 1 < PANELS:
                solved = solve(next_panel[...], 0)
                first_panel[...] = solved
                current[panel + 1, 0] = next_diagonal[:BLOCK, :BLOCK] - dot_nt(solved[:BLOCK], solved[:BLOCK])
                schur[...] = next_diagonal[...] - dot_nt(solved, solved)

    def fill_pending(index, panel):
        row = lower[panel, index * BLOCK : (index + 1) * BLOCK, :]
        head = row.astype(BF16)
        tail = (row - head.astype(F32)).astype(BF16)
        both = jnp.concatenate([head, tail], axis=0)
        product = dot_nn(both, high[panel])
        pending[...] = product[:BLOCK] + product[BLOCK:] + dot_nn(head, low[panel])

    def kept(k, value):
        return jnp.where(ids[3 + k] == row_tile, value, value.astype(BF16).astype(F32))

    parts = NB // BLOCK
    share = 3 * NB // parts

    for index in range(parts):
        near = pl.ds(index * BLOCK, BLOCK)
        start = index * BLOCK
        next_panel[near, :] = offdiagonal_rows(NB + start, BLOCK, 0)
        next_diagonal[near, :] = diagonal_rows(1, start, BLOCK)
        own = index * share
        for panel in range(PANELS):
            covs[panel, pl.ds(own, share), :] = offdiagonal_rows(2 * NB + own, share, panel)
        fill_pending(index, 0)
        unit_inverse[0, index] = inverse_factor(current[0, index])
        stage(0, index)

    for index in range(parts):
        if index < 2:
            same = ids[3 + index] == row_tile
            decay, gain = covariance(2 * NB, NB, (3 + index) * NB)
            decay = jnp.where(own_pairs(0, NB) & same, decay + NUGGET, decay)
            partial[index] = kept(index, decay * gain)
        if index < 3:
            own = pl.ds(index * NB, NB)
            solved = solve(covs[0, own, :], 0)
            panels[0, own, :] = solved
            change = dot_nt(solved, first_panel[...])
            covs[1, own, :] = (covs[1, own, :].astype(F32) - change).astype(BF16)
        else:
            panels[1, :, :half] = half_solve(covs[1, :, :half], 1, 0).astype(BF16)
            for k in range(2):
                change = dot_nt(panels[0, :NB, :], panels[0, (1 + k) * NB : (2 + k) * NB, :])
                partial[k] = kept(k, partial[k] - change)
        fill_pending(index, 1)
        unit_inverse[1, index] = inverse_factor(current[1, index])
        stage(1, index)

    panels[1, :, half:] = half_solve(covs[1], 1, half).astype(BF16)

    for k in range(2):
        tile = ids[3 + k]

        @pl.when((row_tile < PANELS) & (tile > row_tile))
        def _():
            out_ref[:, k, :] = jnp.zeros((NB, NB), BF16)

        @pl.when((row_tile >= PANELS) & (tile >= PANELS))
        def _():
            change = dot_nt(panels[1, :NB, :], panels[1, (1 + k) * NB : (2 + k) * NB, :])
            out_ref[:, k, :] = (partial[k] - change).astype(BF16)

    for panel in range(PANELS):

        @pl.when((col_tile == panel) & (row_tile > panel))
        def _():
            out_ref[:, 0, :] = panels[panel, 0:NB, :]

    for panel in range(PANELS):

        @pl.when(is_factor & (row_tile == panel))
        def _():
            out_ref[:, 0, :] = lower[panel].astype(BF16)
            for p in range(parts):
                span = slice(p * BLOCK, (p + 1) * BLOCK)
                block = dot_nt(current[panel, p], unit_inverse[panel, p], HIGH)
                r = lax.broadcasted_iota(jnp.int32, (BLOCK, BLOCK), 0)
                c = lax.broadcasted_iota(jnp.int32, (BLOCK, BLOCK), 1)
                out_ref[span, 0, span] = jnp.where(c <= r, block, 0.0).astype(BF16)


def device_tiles(place, gathered):
    vmem = pl.BlockSpec(memory_space=pltpu.VMEM)
    return pl.pallas_call(
        tile_kernel,
        out_shape=jax.ShapeDtypeStruct((NB, 2, NB), BF16),
        in_specs=[pl.BlockSpec(memory_space=pltpu.SMEM), vmem],
        out_specs=vmem,
        scratch_shapes=[
            pltpu.VMEM((8, 5 * NB), F32),
            pltpu.VMEM((5 * NB, 8), F32),
            pltpu.VMEM((NB, NB), F32),
            pltpu.VMEM((PANELS, NB, NB), F32),
            pltpu.VMEM((PANELS, NB, NB), BF16),
            pltpu.VMEM((PANELS, NB, NB), BF16),
            pltpu.VMEM((PANELS, NB // BLOCK, BLOCK, BLOCK), F32),
            pltpu.VMEM((PANELS, NB // BLOCK, BLOCK, BLOCK), F32),
            pltpu.VMEM((BLOCK, NB), F32),
            pltpu.VMEM((NB, NB), BF16),
            pltpu.VMEM((NB, NB), BF16),
            pltpu.VMEM((NB, NB), F32),
            pltpu.VMEM((2, NB, NB), F32),
            pltpu.VMEM((PANELS, 3 * NB, NB), BF16),
            pltpu.VMEM((PANELS, 3 * NB, NB), BF16),
        ],
        compiler_params=pltpu.CompilerParams(vmem_limit_bytes=48 * 1024 * 1024),
    )(place, gathered)


def per_device(locations, scales, sample_times):
    core = lax.axis_index("core")
    row_place = lax.axis_index("chip") * 2 + core
    col_place = lax.axis_index("col")
    chips = lax.axis_size("chip")
    kind = lax.broadcasted_iota(jnp.int32, (1, 3, NB), 1)
    codes, times = locations.astype(F32), sample_times.astype(F32)
    own = jnp.where(
        kind == 0, codes[:, None], jnp.where(kind == 1, times[:, None], scales[:, None])
    )
    other = lax.ppermute(own, "core", [(0, 1), (1, 0)])
    pair = jnp.concatenate([own, other], axis=0)
    copies = jnp.broadcast_to(pair[None], (chips,) + pair.shape)
    gathered = lax.all_to_all(copies, "chip", 0, 0, tiled=True)
    gathered = gathered.reshape((2 * chips,) + own.shape[1:])
    place = jnp.stack([row_place, col_place, col_place + lax.axis_size("col"), core])
    tiles = device_tiles(place.astype(jnp.int32), gathered)
    return tiles[None]


def solution(mesh):
    rows, cols = mesh.devices.shape
    split = Mesh(mesh.devices.reshape(rows // 2, 2, cols), ("chip", "core", "col"))
    row = P(None, ("chip", "core"))
    return jax.shard_map(
        per_device,
        mesh=split,
        in_specs=(row, row, row),
        out_specs=P(None, ("chip", "core"), None, "col"),
        check_vma=False,
    )
```
